128 devices in a mesh: seq: 32 (over z, y, core), head: 4 (over x).
Axes of the slice: x: 4, y: 4, z: 4, core: 2. Of those that a mesh axis runs over, the one named last changes fastest.
Arguments:
- tokens: bfloat16 [24576, 5120], P('seq', 'head'), may hold values from -21 to 21
- w_query: bfloat16 [5120, 2560], P('seq', 'head'), may hold values from -0.078125 to 0.078125
- w_key: bfloat16 [5120, 2560], P('seq', 'head'), may hold values from -0.078125 to 0.078125
- w_value: bfloat16 [5120, 2560], P('seq', 'head'), may hold values from -0.078125 to 0.078125
- w_out: bfloat16 [2560, 5120], P(None, ('head', 'seq')), may hold values from -0.125 to 0.125
- frame_lists: int32 [32, 5], P('seq'), may hold values from -1 to 61, as said below
Outputs:
- layer_out: bfloat16 [24576, 5120], P('seq', 'head')
The draws below stay inside these ranges and needn't reach their ends.
Inputs may be any that keep to these rules, and one draw needn't show every extreme that they name: `frame_lists`: row c holds distinct frame numbers, each below 2 * c and either below 1 or at least 2 * c - 4; -1 marks an empty slot. Frame 2 * c - 4 is listed in some row c.
All inputs are finite; a program needn't handle non-finite values.
Results may differ from the reference program's by a relative error of at most 0.012.
The reference program's roundings to bfloat16 on the way (of `queries`, `weights` and `attended`) count: a program that leaves them out, or rounds other values in their place, can miss the bound.
Values may be sent and summed in bfloat16 or wider, within the bound.
No kernel may reach another device: no remote copies, remote signals or barrier semaphores. Data moves between devices by JAX's collectives and lax.ppermute only.
A program may use at most 128 MiB of HBM per device.

```python
import jax
import jax.numpy as jnp
from jax import lax

D = 5120
HEAD_DIM = 128
FT = 384
FPC = 2
SINK = 1
WIN = 4
HEADS = 20
LIST = 5
TOK_DEV = 768
SPANS = 32
FRAMES = 64
TOKENS = 24576


def draw_tokens(key, part):
    key = jax.random.fold_in(key, 23)
    base_key = jax.random.fold_in(key, 0)
    values = jnp.clip(jax.random.normal(base_key, (TOKENS, D), jnp.float32), -6.0, 6.0)
    return values.astype(jnp.bfloat16)


def draw_frame_lists(key, part):
    key = jax.random.fold_in(key, 11)
    width_key, keep_key = jax.random.split(key)
    widths = jax.random.randint(width_key, (SPANS,), 1, WIN + 1)
    widths = widths.at[SPANS - 1].set(WIN)
    widths = widths.at[1].set(WIN)
    widths = widths.at[2].set(WIN)
    keep_sink = jax.random.randint(keep_key, (SPANS, SINK), 0, 4) > 0
    span_ids = jnp.arange(SPANS, dtype=jnp.int32)[:, None]
    first_frame = span_ids * FPC
    sink_ids = jnp.arange(SINK, dtype=jnp.int32)[None, :]
    sinks = jnp.where(keep_sink & (sink_ids < first_frame), sink_ids, -1)
    offsets = jnp.arange(1, WIN + 1, dtype=jnp.int32)[None, :]
    window_ids = first_frame - offsets
    window_ok = (offsets <= widths[:, None]) & (window_ids >= SINK)
    windows = jnp.where(window_ok, window_ids, -1)
    return jnp.concatenate([sinks, windows], axis=1).astype(jnp.int32)


def levels(key, dims, shards, low, top_value):
    factor_of, own = 1.0, jax.random.fold_in(key, 6)
    for dim, parts in shards:
        steps = jnp.exp(jax.random.uniform(jax.random.fold_in(own, dim), (parts,), jnp.float32, low / len(shards), top_value / len(shards)))
        factor_of = factor_of * jnp.repeat(steps, dims[dim] // parts).reshape([-1 if axis == dim else 1 for axis in range(len(dims))])
    return factor_of


def centred(rng, dims, width, limit, shards=(), held_as=jnp.bfloat16):
    loudness = levels(rng, dims, shards, -0.22, 0.18) if shards else 1.0
    values = jax.random.normal(rng, dims, jnp.float32) * width * loudness
    return jnp.minimum(jnp.maximum(values, -limit), limit).astype(held_as)


def setup_inputs(seed: int = 0) -> dict:
    keys = jax.random.split(jax.random.key(seed), 7)
    tokens = draw_tokens(jax.random.fold_in(keys[6], 71), 0)
    w_query = centred(keys[1], (D, HEADS * HEAD_DIM), D ** -0.5, 0.078125, ((0, 32), (1, 4)))
    w_key = centred(keys[2], (D, HEADS * HEAD_DIM), D ** -0.5, 0.078125, ((0, 32), (1, 4)))
    w_value = centred(keys[3], (D, HEADS * HEAD_DIM), D ** -0.5, 0.078125, ((0, 32), (1, 4)))
    w_out = centred(keys[4], (HEADS * HEAD_DIM, D), (HEADS * HEAD_DIM) ** -0.5, 0.125, ((1, 128),))
    frame_lists = draw_frame_lists(jax.random.fold_in(keys[6], 71), 0)
    return dict(tokens=tokens, w_query=w_query, w_key=w_key, w_value=w_value, w_out=w_out, frame_lists=frame_lists)


def reference(tokens, w_query, w_key, w_value, w_out, frame_lists):
    queries = jnp.dot(tokens, w_query, preferred_element_type=jnp.float32).astype(jnp.bfloat16)
    key_proj = jnp.dot(tokens, w_key, preferred_element_type=jnp.float32).astype(jnp.bfloat16)
    value_proj = jnp.dot(tokens, w_value, preferred_element_type=jnp.float32).astype(jnp.bfloat16)
    key_frames = key_proj.reshape(FRAMES, FT, HEADS, HEAD_DIM)
    value_frames = value_proj.reshape(FRAMES, FT, HEADS, HEAD_DIM)
    query_spans = queries.reshape(SPANS, TOK_DEV, HEADS, HEAD_DIM)
    own_keys = key_proj.reshape(SPANS, TOK_DEV, HEADS, HEAD_DIM)
    own_values = value_proj.reshape(SPANS, TOK_DEV, HEADS, HEAD_DIM)
    scale = 1.0 / (HEAD_DIM ** 0.5)

    def one_span(operands):
        query_block, key_block, value_block, listed = operands
        slots = jnp.maximum(listed, 0).astype(jnp.int32)
        listed_keys = key_frames[slots].reshape(LIST * FT, HEADS, HEAD_DIM)
        listed_values = value_frames[slots].reshape(LIST * FT, HEADS, HEAD_DIM)
        valid = jnp.repeat(listed >= 0, FT)
        key_all = jnp.concatenate([key_block, listed_keys], axis=0).astype(jnp.float32)
        value_all = jnp.concatenate([value_block, listed_values], axis=0).astype(jnp.float32)
        allowed = jnp.concatenate([jnp.ones((TOK_DEV,), bool), valid])
        scores = jnp.einsum("qhd,khd->hqk", query_block.astype(jnp.float32), key_all) * scale
        scores = jnp.where(allowed[None, None, :], scores, jnp.float32(-1e30))
        row_peak = jnp.max(scores, axis=-1, keepdims=True)
        powers = jnp.exp(scores - row_peak)
        totals = jnp.sum(powers, axis=-1)
        weights = powers.astype(jnp.bfloat16).astype(jnp.float32)
        blended = jnp.einsum("hqk,khd->qhd", weights, value_all) / jnp.transpose(totals)[:, :, None]
        return blended.astype(jnp.bfloat16).reshape(TOK_DEV, HEADS * HEAD_DIM)

    attended = lax.map(one_span, (query_spans, own_keys, own_values, frame_lists))
    attended = attended.reshape(TOKENS, HEADS * HEAD_DIM)
    return jnp.dot(attended, w_out, preferred_element_type=jnp.float32).astype(jnp.bfloat16)
```

```python
import math

import jax
import jax.numpy as jnp
from jax import lax
from jax.experimental import pallas as pl
from jax.experimental.pallas import tpu as pltpu
from jax.sharding import PartitionSpec as P

HEAD_DIM = 128
FT = 384
SINK = 1
AXES = ("seq", "head")
N_DEV = 128
GROUP = 640
FEAT = 1280
EXP_SCALE = math.log2(math.e) / math.sqrt(HEAD_DIM)
ABSENT = 1e30
BF = jnp.bfloat16
VMEM_LIMIT = 60 * 1024 * 1024


def place(i):
    seq, x = divmod(i, 4)
    z, rest = divmod(seq, 8)
    y, core = divmod(rest, 2)
    return z, y, core, x


def index(z, y, core, x):
    return (((z % 4) * 4 + y % 4) * 2 + core % 2) * 4 + x % 4


def move(value, target):
    pairs = []
    for i in range(N_DEV):
        to = target(*place(i))
        if to is not None:
            pairs.append((i, index(*to)))
    return lax.ppermute(value, AXES, pairs)


def along_x(value, steps):
    return move(value, lambda z, y, c, x: (z, y, c, x + steps))


def swap_cores(value):
    return move(value, lambda z, y, c, x: (z, y, 1 - c, x))


def spans_on(value, spans):
    pairs = [(i, i + 4 * spans) for i in range(N_DEV - 4 * spans)]
    return lax.ppermute(value, AXES, pairs)


def after(value, other):
    return value + other[0, 0] * jnp.zeros((), value.dtype)


def x_ring(first, second):
    first_a = along_x(first, 1)
    first_b = along_x(first, -1)
    first_c = along_x(first_a, 1)
    second_b = along_x(after(second, first_b), -1)
    second_c = along_x(second_b, -1)
    second_a = along_x(after(second, first_c), 1)
    return (first_a, first_b, first_c), (second_a, second_b, second_c)


def parity_gather(value):
    groups = [[2 * i for i in range(16)], [2 * i + 1 for i in range(16)]]
    own = lax.all_gather(value, "seq", axis=0, tiled=True, axis_index_groups=groups)
    return own, swap_cores(own)


def spread_sink(key_value, z, y, core):
    at_start = lambda zz, yy: zz == 0 and yy == 0
    to_core1 = move(
        key_value[:, GROUP:],
        lambda zz, yy, c, x: (zz, yy, 1, x) if at_start(zz, yy) and c == 0 else None,
    )
    half = jnp.where(core == 0, key_value[:, :GROUP], to_core1)

    def stage(value, first):
        def hop(origin, steps):
            def target(zz, yy, c, x):
                by_z = (c == 0) == first
                here, cross = (zz, yy) if by_z else (yy, zz)
                if here != origin or (first and cross != 0):
                    return None
                return (zz + steps, yy, c, x) if by_z else (zz, yy + steps, c, x)

            return target

        up = move(value, hop(0, 1))
        down = move(value, hop(0, -1))
        far = move(up, hop(1, 1))
        mine = jnp.where((core == 0) == first, z, y)
        return jnp.where(
            mine == 0, value, jnp.where(mine == 1, up, jnp.where(mine == 3, down, far))
        )

    half = stage(stage(half, True), False)
    other = swap_cores(half)
    sink_key = jnp.where(core == 0, half, other)
    sink_value = jnp.where(core == 0, other, half)
    return sink_key, sink_value


def project_kernel(chunks, columns, where_ref, *refs):
    tokens_ref = refs[0]
    pieces = refs[1 : 1 + 3 * chunks]
    own_ref, other_ref = refs[1 + 3 * chunks : 3 + 3 * chunks]
    out_ref, feat, weights, feat_sem, weight_sem = refs[3 + 3 * chunks :]
    x, core, base = where_ref[0], where_ref[1], where_ref[2]
    order = [x, lax.rem(x + 3, 4), lax.rem(x + 1, 4), lax.rem(x + 2, 4)]
    copies = []
    for k in range(chunks):
        start = base if chunks == 1 else k * FT
        rows = pl.ds(pl.multiple_of(start, FT), FT)
        sources = [tokens_ref.at[rows, :]] + list(pieces[3 * k : 3 * k + 3])
        for j, source in enumerate(sources):
            copies.append(
                pltpu.make_async_copy(
                    source, feat.at[order[j], pl.ds(k * FT, FT), :], feat_sem.at[4 * k + j]
                )
            )
    width = columns // GROUP
    loads = []
    for n in range(width):
        for g in range(4):
            for h, source in enumerate((own_ref, other_ref)):
                side = core if h == 0 else 1 - core
                loads.append(
                    pltpu.make_async_copy(
                        source.at[pl.ds(4 * g, 4), :, pl.ds(n * GROUP, GROUP)],
                        weights.at[n, pl.ds(4 * g, 4), side],
                        weight_sem.at[(n * 4 + g) * 2 + h],
                    )
                )
    for copy in copies:
        copy.start()
    for load in loads:
        load.start()
    for copy in copies:
        copy.wait()
    for n in range(width):
        total = None
        for g in range(4):
            loads[(n * 4 + g) * 2].wait()
            loads[(n * 4 + g) * 2 + 1].wait()
            block = weights[n, 4 * g : 4 * g + 4].reshape(FEAT, GROUP)
            part = jnp.dot(feat[g], block, preferred_element_type=jnp.float32)
            total = part if total is None else total + part
        out_ref[:, n * GROUP : (n + 1) * GROUP] = total.astype(BF)


def project(where, tokens, ring, own, other):
    chunks = len(ring)
    columns = own.shape[1]
    width = columns // GROUP
    anywhere = pl.BlockSpec(memory_space=pl.ANY)
    pieces = [piece for chunk in ring for piece in chunk]
    rows = chunks * FT

    def kernel(*refs):
        project_kernel(chunks, columns, *refs)

    return pl.pallas_call(
        kernel,
        out_shape=jax.ShapeDtypeStruct((rows, columns), BF),
        in_specs=[pl.BlockSpec(memory_space=pltpu.SMEM)] + [anywhere] * (len(pieces) + 3),
        out_specs=pl.BlockSpec(memory_space=pltpu.VMEM),
        scratch_shapes=[
            pltpu.VMEM((4, rows, FEAT), BF),
            pltpu.VMEM((width, 16, 2, 160, GROUP), BF),
            pltpu.SemaphoreType.DMA((4 * chunks,)),
            pltpu.SemaphoreType.DMA((8 * width,)),
        ],
        compiler_params=pltpu.CompilerParams(vmem_limit_bytes=VMEM_LIMIT),
        name="project",
    )(where, tokens, *pieces, own.reshape(16, 160, columns), other.reshape(16, 160, columns))


def attend_kernel(penalty_ref, query_ref, *refs):
    keys, values, out_ref = refs[:7], refs[7:14], refs[14]
    query = query_ref[...]
    lanes = HEAD_DIM
    scores = []
    peak = None
    for f in range(7):
        s = lax.dot_general(
            query, keys[f][...], (((1,), (1,)), ((), ())), preferred_element_type=jnp.float32
        )
        scores.append(s)
        top = jnp.maximum(
            jnp.maximum(s[:, :lanes], s[:, lanes : 2 * lanes]), s[:, 2 * lanes :]
        )
        if f >= 2:
            top = top - penalty_ref[f]
        peak = top if peak is None else jnp.maximum(peak, top)
    row_peak = jnp.max(peak, axis=1, keepdims=True) * EXP_SCALE
    totals = None
    blended = None
    for f in range(7):
        shift = row_peak if f < 2 else row_peak + penalty_ref[f]
        powers = jnp.exp2(scores[f] * EXP_SCALE - shift)
        part = powers[:, :lanes] + powers[:, lanes : 2 * lanes] + powers[:, 2 * lanes :]
        totals = part if totals is None else totals + part
        more = jnp.dot(powers.astype(BF), values[f][...], preferred_element_type=jnp.float32)
        blended = more if blended is None else blended + more
    total = jnp.sum(totals, axis=1, keepdims=True)
    out_ref[...] = (blended / total).astype(BF)


def attend(penalty, queries, chunk, frames, sink_key, sink_value):
    def columns(first):
        return pl.BlockSpec((FT, HEAD_DIM), lambda h: (0, first + h))

    own = list(frames[:2])
    window = list(frames[2:])
    key_arrays = own + [sink_key] + window
    value_arrays = own + [sink_value] + window
    key_specs = [columns(0)] * 7
    value_specs = [columns(5)] * 2 + [columns(0)] + [columns(5)] * 4
    return pl.pallas_call(
        attend_kernel,
        grid=(5,),
        out_shape=jax.ShapeDtypeStruct((FT, GROUP), BF),
        in_specs=[
            pl.BlockSpec(memory_space=pltpu.SMEM),
            pl.BlockSpec((FT, HEAD_DIM), lambda h: (chunk, h)),
        ]
        + key_specs
        + value_specs,
        out_specs=columns(0),
        compiler_params=pltpu.CompilerParams(vmem_limit_bytes=VMEM_LIMIT),
        name="attend",
    )(penalty, queries, *key_arrays, *value_arrays)


def output_kernel(where_ref, own_ref, a_ref, b_ref, c_ref, w_ref, out_ref, feat, sem):
    x = where_ref[0]
    order = [x, lax.rem(x + 3, 4), lax.rem(x + 1, 4), lax.rem(x + 2, 4)]
    copies = [
        pltpu.make_async_copy(source, feat.at[order[j]], sem.at[j])
        for j, source in enumerate((own_ref, a_ref, b_ref, c_ref))
    ]
    for copy in copies:
        copy.start()
    for copy in copies:
        copy.wait()
    total = None
    for g in range(4):
        part = lax.dot_general(
            feat[g],
            w_ref[:, g * GROUP : (g + 1) * GROUP],
            (((1,), (1,)), ((), ())),
            preferred_element_type=jnp.float32,
        )
        total = part if total is None else total + part
    out_ref[...] = total.astype(BF)


def output_rows(where, own, ring, weights):
    anywhere = pl.BlockSpec(memory_space=pl.ANY)
    return pl.pallas_call(
        output_kernel,
        out_shape=jax.ShapeDtypeStruct((FT, FEAT), BF),
        in_specs=[pl.BlockSpec(memory_space=pltpu.SMEM)]
        + [anywhere] * 4
        + [pl.BlockSpec(memory_space=pltpu.VMEM)],
        out_specs=pl.BlockSpec(memory_space=pltpu.VMEM),
        scratch_shapes=[pltpu.VMEM((4, FT, GROUP), BF), pltpu.SemaphoreType.DMA((4,))],
        compiler_params=pltpu.CompilerParams(vmem_limit_bytes=VMEM_LIMIT),
        name="output_rows",
    )(where, own, *ring, weights)


def penalties(span, listed):
    ids = span * 2 + jnp.array([0, 1, 0, -2, -1, -4, -3], jnp.int32)
    ids = ids.at[2].set(0)
    found = jnp.any(ids[:, None] == listed[None, :], axis=1)
    slot = jnp.arange(7)
    allowed = (slot < 2) | (found & ((slot == 2) | (ids >= SINK)))
    return jnp.where(allowed, 0.0, ABSENT).astype(jnp.float32)


def local(tokens, w_query, w_key, w_value, w_out, frame_lists):
    span = lax.axis_index("seq")
    x = lax.axis_index("head")
    z, y, core = span // 8, span // 2 % 4, span % 2
    penalty = penalties(span, frame_lists[0])

    ring_first, ring_second = x_ring(tokens[:FT], tokens[FT:])
    kv_own, kv_other = parity_gather(jnp.concatenate([w_key, w_value], axis=1))
    q_own, q_other = parity_gather(w_query)
    out_own, out_other = parity_gather(w_out.T)

    def where(base):
        return jnp.stack([x, core, jnp.int32(base)]).astype(jnp.int32)

    kv_first = project(where(0), tokens, [ring_first], kv_own, kv_other)
    kv_second = project(where(FT), tokens, [ring_second], kv_own, kv_other)
    sink_key, sink_value = spread_sink(kv_first, z, y, core)
    frames = [kv_first, kv_second]
    near, far = [], []
    for mine in (kv_first, kv_second):
        distant = spans_on(mine, 2)
        far.append(distant)
        near.append(swap_cores(jnp.where(core == 0, mine, distant)))
    frames = frames + near + far
    queries = project(where(0), tokens, [ring_first, ring_second], q_own, q_other)

    att_first = attend(penalty, queries, 0, frames, sink_key, sink_value)
    att_second = attend(penalty, queries, 1, frames, sink_key, sink_value)
    got_first, got_second = x_ring(att_first, att_second)

    blocks = [out_own.reshape(16, 40, 2560), out_other.reshape(16, 40, 2560)]
    even = jnp.where(core == 0, blocks[0], blocks[1])
    odd = jnp.where(core == 0, blocks[1], blocks[0])
    out_weights = jnp.stack([even, odd], axis=1).reshape(FEAT, 2560)
    out_first = output_rows(where(0), att_first, got_first, out_weights)
    out_second = output_rows(where(0), att_second, got_second, out_weights)
    return jnp.concatenate([out_first, out_second], axis=0)


def solution(mesh):
    placed = (
        P("seq", "head"),
        P("seq", "head"),
        P("seq", "head"),
        P("seq", "head"),
        P(None, ("head", "seq")),
        P("seq", None),
    )
    return jax.shard_map(
        local, mesh=mesh, in_specs=placed, out_specs=P("seq", "head"), check_vma=False
    )
```

```python
import math

import jax
import jax.numpy as jnp
from jax import lax
from jax.experimental import pallas as pl
from jax.experimental.pallas import tpu as pltpu
from jax.sharding import PartitionSpec as P

HEAD_DIM = 128
FT = 384
SINK = 1
AXES = ("seq", "head")
N_DEV = 128
GROUP = 640
FEAT = 1280
EXP_SCALE = math.log2(math.e) / math.sqrt(HEAD_DIM)
ABSENT = 1e30
BF = jnp.bfloat16
VMEM_LIMIT = 60 * 1024 * 1024
SIZES = (3, 2)


def place(i):
    seq, x = divmod(i, 4)
    z, rest = divmod(seq, 8)
    y, core = divmod(rest, 2)
    return z, y, core, x


def index(z, y, core, x):
    return (((z % 4) * 4 + y % 4) * 2 + core % 2) * 4 + x % 4


def move(value, target):
    pairs = []
    for i in range(N_DEV):
        to = target(*place(i))
        if to is not None:
            pairs.append((i, index(*to)))
    return lax.ppermute(value, AXES, pairs)


def along_x(value, steps):
    return move(value, lambda z, y, c, x: (z, y, c, x + steps))


def swap_cores(value):
    return move(value, lambda z, y, c, x: (z, y, 1 - c, x))


def spans_on(value, spans):
    pairs = [(i, i + 4 * spans) for i in range(N_DEV - 4 * spans)]
    return lax.ppermute(value, AXES, pairs)


def after(value, other):
    return value + other[0, 0] * jnp.zeros((), value.dtype)


def x_ring(value, core):
    left = along_x(value, 1)
    right = along_x(value, -1)
    far = move(
        jnp.where(core == 0, left, right),
        lambda z, y, c, x: (z, y, c, x + 1 if c == 0 else x - 1),
    )
    return left, right, far


def parity_gather(value):
    groups = [[2 * i for i in range(16)], [2 * i + 1 for i in range(16)]]
    own = lax.all_gather(value, "seq", axis=0, tiled=True, axis_index_groups=groups)
    return own, swap_cores(own)


SINK_ROWS = 16


def scatter_sink(tokens, span, gate):
    padded = jnp.pad(tokens[:FT], ((0, 32 * SINK_ROWS - FT), (0, 0)))
    padded = jnp.where(span == 0, padded, jnp.zeros_like(padded))
    rows = lax.psum_scatter(padded, "seq", scatter_dimension=0, tiled=True)
    rows = after(rows, gate)
    return [rows] + [along_x(rows, steps) for steps in (3, 2, 1)]


OFFSETS = (0, -1, 1, 2)


def weight_ring(value):
    def hop(value, first, steps):
        return move(
            value,
            lambda z, y, c, x: (z, y + steps, c, x)
            if (c == 0) == first
            else (z + steps, y, c, x),
        )

    def stage(value, first):
        half = value.shape[0] // 2
        up = hop(value, first, 1)
        down = hop(value, first, -1)
        return up, down, hop(up[:half], first, 1), hop(down[half:], first, -1)

    line = jnp.concatenate([value, *stage(value, True)], axis=0)
    return (line, *stage(line, False))


def ring_blocks(pieces, z, y, z_first):
    line, up, down, far_top, far_bottom = pieces
    for i, source in enumerate((line, up, down, None)):
        for k in range(4):
            ref, row = source, 160 * k
            if i == 3:
                ref, row = (far_top, 160 * k) if k < 2 else (far_bottom, 160 * (k - 2))
            dz = OFFSETS[i] + z_first * (OFFSETS[k] - OFFSETS[i])
            dy = OFFSETS[k] + z_first * (OFFSETS[i] - OFFSETS[k])
            yield ref, row, lax.rem(z + dz + 4, 4), lax.rem(y + dy + 4, 4)


def gather_blocks(pieces, z, y, z_first):
    for i in range(16):
        yield pieces[0], 160 * i, i // 4, i % 4


def project(where, features, extra, own, other, blocks_of, groups, splits):
    columns = own[0].shape[1]
    rows = 2 * FT
    count = len(own)
    pieces = [features[g] for g in groups]
    extras = [] if extra is None else [extra[g] for g in groups]
    all_rows = rows + SINK_ROWS * bool(extras)
    anywhere = pl.BlockSpec(memory_space=pl.ANY)
    whole = pl.BlockSpec(memory_space=pltpu.VMEM)

    def kernel(where_ref, *refs):
        piece_refs, refs = refs[: len(pieces)], refs[len(pieces) :]
        sides, refs = (refs[:count], refs[count : 2 * count]), refs[2 * count :]
        extra_refs, refs = refs[: len(extras)], refs[len(extras) :]
        out_refs, (feat, weights, sums, feat_sem, weight_sem) = refs[:-5], refs[-5:]
        x, core, z, y = where_ref[0], where_ref[1], where_ref[2], where_ref[3]

        copies = []
        for n, ref in enumerate(piece_refs):
            mine = [pltpu.make_async_copy(ref, feat.at[n, pl.ds(0, rows), :], feat_sem.at[n, 0])]
            if extras:
                mine.append(
                    pltpu.make_async_copy(
                        extra_refs[n], feat.at[n, pl.ds(rows, SINK_ROWS), :], feat_sem.at[n, 1]
                    )
                )
            for copy in mine:
                copy.start()
            copies.append(mine)
        for h in range(2):
            side = core if h == 0 else 1 - core
            for ref, row, bz, by in blocks_of(sides[h], z, y, side):
                ahead = lax.rem(bz - x + 4, 4)
                for n, g in enumerate(groups):

                    @pl.when(ahead == g)
                    def _():
                        pltpu.make_async_copy(
                            ref.at[pl.ds(row, 160), :],
                            weights.at[n, by, side],
                            weight_sem.at[n, by, side],
                        ).start()

        for n in range(len(groups)):
            for copy in copies[n]:
                copy.wait()
            for by in range(4):
                for side in range(2):
                    pltpu.make_async_copy(
                        sides[0][0].at[pl.ds(0, 160), :],
                        weights.at[n, by, side],
                        weight_sem.at[n, by, side],
                    ).wait()
            part = jnp.dot(
                feat[n], weights[n].reshape(FEAT, columns), preferred_element_type=jnp.float32
            )
            if n:
                part = part + sums[...]
            if n < len(groups) - 1:
                sums[...] = part
        out_refs[0][...] = part[:rows].astype(BF)
        if extras:
            out_refs[-1][...] = part[rows:].astype(BF)
        for ref, parts in zip(out_refs[1:], splits):
            at = 0
            for start, stop in parts:
                ref[:, at : at + stop - start] = out_refs[0][:, start:stop]
                at += stop - start

    shapes = [jax.ShapeDtypeStruct((rows, columns), BF)] + [
        jax.ShapeDtypeStruct((rows, sum(stop - start for start, stop in parts)), BF)
        for parts in splits
    ]
    if extras:
        shapes.append(jax.ShapeDtypeStruct((SINK_ROWS, columns), BF))
    return pl.pallas_call(
        kernel,
        out_shape=shapes,
        in_specs=[pl.BlockSpec(memory_space=pltpu.SMEM)]
        + [anywhere] * (len(pieces) + 2 * count + len(extras)),
        out_specs=[whole] * len(shapes),
        scratch_shapes=[
            pltpu.VMEM((len(groups), all_rows, FEAT), BF),
            pltpu.VMEM((len(groups), 4, 2, 160, columns), BF),
            pltpu.VMEM((all_rows, columns), jnp.float32),
            pltpu.SemaphoreType.DMA((len(pieces), 2)),
            pltpu.SemaphoreType.DMA((len(groups), 4, 2)),
        ],
        compiler_params=pltpu.CompilerParams(vmem_limit_bytes=VMEM_LIMIT),
        name="project",
    )(where, *pieces, *own, *other, *extras)


def attend_kernel(penalty_ref, query_ref, *refs):
    query = query_ref[...]
    lanes = HEAD_DIM
    keys, values = [], []
    for key_ref, value_ref in zip(refs[:4], refs[4:8]):
        for start in range(0, key_ref.shape[0], FT):
            keys.append((key_ref, start))
            values.append((value_ref, start))
    out_ref = refs[8]
    scores = []
    peak = None
    for f, (ref, start) in enumerate(keys):
        s = lax.dot_general(
            query,
            ref[start : start + FT, :],
            (((1,), (1,)), ((), ())),
            preferred_element_type=jnp.float32,
        )
        scores.append(s)
        top = jnp.maximum(
            jnp.maximum(s[:, :lanes], s[:, lanes : 2 * lanes]), s[:, 2 * lanes :]
        )
        if f >= 2:
            top = top - penalty_ref[f]
        peak = top if peak is None else jnp.maximum(peak, top)
    row_peak = jnp.max(peak, axis=1, keepdims=True) * EXP_SCALE
    totals = None
    blended = None
    for f, (ref, start) in enumerate(values):
        shift = row_peak if f < 2 else row_peak + penalty_ref[f]
        powers = jnp.exp2(scores[f] * EXP_SCALE - shift)
        part = powers[:, :lanes] + powers[:, lanes : 2 * lanes] + powers[:, 2 * lanes :]
        totals = part if totals is None else totals + part
        more = jnp.dot(
            powers.astype(BF), ref[start : start + FT, :], preferred_element_type=jnp.float32
        )
        blended = more if blended is None else blended + more
    total = jnp.sum(totals, axis=1, keepdims=True)
    out_ref[...] = (blended / total).astype(BF)


def attend(penalty, first, count, queries, key_value, sink, near, far):
    def columns(rows, begin):
        return pl.BlockSpec((rows, HEAD_DIM), lambda h: (0, begin + h))

    rows = 2 * FT
    return pl.pallas_call(
        attend_kernel,
        grid=(count,),
        out_shape=jax.ShapeDtypeStruct((rows, count * HEAD_DIM), BF),
        in_specs=[
            pl.BlockSpec(memory_space=pltpu.SMEM),
            columns(rows, first),
            columns(rows, first),
            columns(FT, first),
            columns(rows, 0),
            columns(rows, 0),
            columns(rows, 5 + first),
            columns(FT, 5 + first),
            columns(rows, count),
            columns(rows, count),
        ],
        out_specs=columns(rows, 0),
        compiler_params=pltpu.CompilerParams(vmem_limit_bytes=VMEM_LIMIT),
        name="attend",
    )(
        penalty,
        queries,
        key_value,
        sink,
        near,
        far,
        key_value,
        sink,
        near,
        far,
    )


def output(where, first, count, own, ring, weights, total, last):
    rows, width = 2 * FT, count * HEAD_DIM
    anywhere = pl.BlockSpec(memory_space=pl.ANY)
    whole = pl.BlockSpec(memory_space=pltpu.VMEM)
    totals = [] if total is None else [total]

    def kernel(where_ref, own_ref, left_ref, right_ref, far_ref, w_ref, *refs):
        total_refs, (out_ref, feat, weight, feat_sem, weight_sem) = refs[:-5], refs[-5:]
        x = where_ref[0]
        copies = []
        for g, ref in ((0, own_ref), (3, left_ref), (1, right_ref), (2, far_ref)):
            copy = pltpu.make_async_copy(ref, feat.at[g], feat_sem.at[g])
            copy.start()
            copies.append((g, copy))
        loads = []
        for g in range(4):
            begin = lax.rem(x + g, 4) * GROUP + first * HEAD_DIM
            load = pltpu.make_async_copy(
                w_ref.at[:, pl.ds(pl.multiple_of(begin, HEAD_DIM), width)], weight.at[g], weight_sem.at[g]
            )
            load.start()
            loads.append(load)
        result = None
        for g in (0, 3, 1, 2):
            for at, copy in copies:
                if at == g:
                    copy.wait()
            loads[g].wait()
            part = lax.dot_general(
                feat[g], weight[g], (((1,), (1,)), ((), ())), preferred_element_type=jnp.float32
            )
            result = part if result is None else result + part
        if totals:
            result = result + total_refs[0][...]
        out_ref[...] = result.astype(out_ref.dtype)

    return pl.pallas_call(
        kernel,
        out_shape=jax.ShapeDtypeStruct((rows, FEAT), BF if last else jnp.float32),
        in_specs=[pl.BlockSpec(memory_space=pltpu.SMEM)] + [anywhere] * 5 + [whole] * len(totals),
        out_specs=whole,
        scratch_shapes=[
            pltpu.VMEM((4, rows, width), BF),
            pltpu.VMEM((4, FEAT, width), BF),
            pltpu.SemaphoreType.DMA((4,)),
            pltpu.SemaphoreType.DMA((4,)),
        ],
        compiler_params=pltpu.CompilerParams(vmem_limit_bytes=VMEM_LIMIT),
        name="output",
    )(where, own, *ring, weights, *totals)


def penalties(span, listed):
    ids = span * 2 + jnp.array([0, 1, 0, -2, -1, -4, -3], jnp.int32)
    ids = ids.at[2].set(0)
    found = jnp.any(ids[:, None] == listed[None, :], axis=1)
    slot = jnp.arange(7)
    allowed = (slot < 2) | (found & ((slot == 2) | (ids >= SINK)))
    return jnp.where(allowed, 0.0, ABSENT).astype(jnp.float32)


def local(tokens, w_query, w_key, w_value, w_out, frame_lists):
    span = lax.axis_index("seq")
    x = lax.axis_index("head")
    z, y, core = span // 8, span // 2 % 4, span % 2
    penalty = penalties(span, frame_lists[0])

    where = jnp.stack([x, core, z, y]).astype(jnp.int32)

    left, right, far = x_ring(tokens, core)
    sink_tokens = scatter_sink(tokens, span, far)
    features = {0: tokens, 1: right, 2: far, 3: left}
    kv_own = weight_ring(jnp.concatenate([w_key, w_value], axis=1))
    kv_other = [swap_cores(piece) for piece in kv_own]
    q_own, q_other = parity_gather(w_query)
    out_own, out_other = parity_gather(w_out.T)

    ends = [sum(SIZES[: n + 1]) for n in range(len(SIZES))]
    groups = [(end - size, size) for end, size in zip(ends, SIZES)]
    splits = [
        [
            (start * HEAD_DIM, (start + size) * HEAD_DIM),
            (GROUP + start * HEAD_DIM, GROUP + (start + size) * HEAD_DIM),
        ]
        for start, size in groups
    ]
    key_value, *sends, sink_part = project(
        where, features, sink_tokens, kv_own, kv_other, ring_blocks, (0, 1, 3, 2), splits
    )
    (queries,) = project(
        where, features, None, [q_own], [q_other], gather_blocks, (0, 1, 2, 3), ()
    )
    windows = []
    far = None
    for mine in sends:
        if far is not None:
            mine = after(mine, queries)
        far = spans_on(mine, 2)
        near = swap_cores(jnp.where(core == 0, mine, far))
        windows.append((near, far))
    sink = lax.all_gather(sink_part, "seq", axis=0, tiled=True)
    blocks = [out_own.reshape(16, 40, 2560), out_other.reshape(16, 40, 2560)]
    even = jnp.where(core == 0, blocks[0], blocks[1])
    odd = jnp.where(core == 0, blocks[1], blocks[0])
    out_weights = jnp.stack([even, odd], axis=1).reshape(FEAT, 2560)

    total = None
    ring = None
    for n, (start, size) in enumerate(groups):
        near, far = windows[n]
        attended = attend(
            penalty, start, size, queries, key_value, sink, near, far
        )
        if ring is not None:
            attended = after(attended, ring[0])
        ring = x_ring(attended, core)
        total = output(where, start, size, attended, ring, out_weights, total, n == len(groups) - 1)
    return total


def solution(mesh):
    placed = (
        P("seq", "head"),
        P("seq", "head"),
        P("seq", "head"),
        P("seq", "head"),
        P(None, ("head", "seq")),
        P("seq", None),
    )
    return jax.shard_map(
        local, mesh=mesh, in_specs=placed, out_specs=P("seq", "head"), check_vma=False
    )
```

```python
import math

import jax
import jax.numpy as jnp
from jax import lax
from jax.experimental import pallas as pl
from jax.experimental.pallas import tpu as pltpu
from jax.sharding import PartitionSpec as P

HEAD_DIM = 128
FT = 384
SINK = 1
AXES = ("seq", "head")
N_DEV = 128
GROUP = 640
FEAT = 1280
EXP_SCALE = math.log2(math.e) / math.sqrt(HEAD_DIM)
ABSENT = 1e30
BF = jnp.bfloat16
VMEM_LIMIT = 60 * 1024 * 1024
SIZES = (3, 2)


def place(i):
    seq, x = divmod(i, 4)
    z, rest = divmod(seq, 8)
    y, core = divmod(rest, 2)
    return z, y, core, x


def index(z, y, core, x):
    return (((z % 4) * 4 + y % 4) * 2 + core % 2) * 4 + x % 4


def move(value, target):
    pairs = []
    for i in range(N_DEV):
        to = target(*place(i))
        if to is not None:
            pairs.append((i, index(*to)))
    return lax.ppermute(value, AXES, pairs)


def along_x(value, steps):
    return move(value, lambda z, y, c, x: (z, y, c, x + steps))


def swap_cores(value):
    return move(value, lambda z, y, c, x: (z, y, 1 - c, x))


def spans_on(value, spans):
    pairs = [(i, i + 4 * spans) for i in range(N_DEV - 4 * spans)]
    return lax.ppermute(value, AXES, pairs)


def after(value, other):
    return value + other[0, 0] * jnp.zeros((), value.dtype)


def x_ring(value, core):
    left = along_x(value, 1)
    right = along_x(value, -1)
    far = move(
        jnp.where(core == 0, left, right),
        lambda z, y, c, x: (z, y, c, x + 1 if c == 0 else x - 1),
    )
    return left, right, far


def parity_gather(value):
    groups = [[2 * i for i in range(16)], [2 * i + 1 for i in range(16)]]
    own = lax.all_gather(value, "seq", axis=0, tiled=True, axis_index_groups=groups)
    return own, swap_cores(own)


SINK_ROWS = 16


def scatter_sink(tokens, span, gate):
    padded = jnp.pad(tokens[:FT], ((0, 32 * SINK_ROWS - FT), (0, 0)))
    padded = jnp.where(span == 0, padded, jnp.zeros_like(padded))
    rows = lax.psum_scatter(padded, "seq", scatter_dimension=0, tiled=True)
    rows = after(rows, gate)
    return [rows] + [along_x(rows, steps) for steps in (3, 2, 1)]


OFFSETS = (0, -1, 1, 2)


def weight_ring(value):
    def hop(value, first, steps):
        return move(
            value,
            lambda z, y, c, x: (z, y + steps, c, x)
            if (c == 0) == first
            else (z + steps, y, c, x),
        )

    def stage(value, first):
        half = value.shape[0] // 2
        up = hop(value, first, 1)
        down = hop(value, first, -1)
        return up, down, hop(up[:half], first, 1), hop(down[half:], first, -1)

    line = jnp.concatenate([value, *stage(value, True)], axis=0)
    return (line, *stage(line, False))


def ring_blocks(pieces, z, y, z_first):
    line, up, down, far_top, far_bottom = pieces
    for i, source in enumerate((line, up, down, None)):
        for k in range(4):
            ref, row = source, 160 * k
            if i == 3:
                ref, row = (far_top, 160 * k) if k < 2 else (far_bottom, 160 * (k - 2))
            dz = OFFSETS[i] + z_first * (OFFSETS[k] - OFFSETS[i])
            dy = OFFSETS[k] + z_first * (OFFSETS[i] - OFFSETS[k])
            yield ref, row, lax.rem(z + dz + 4, 4), lax.rem(y + dy + 4, 4)


def gather_blocks(pieces, z, y, z_first):
    for i in range(16):
        yield pieces[0], 160 * i, i // 4, i % 4


def project(where, features, extra, own, other, blocks_of, groups, splits):
    columns = own[0].shape[1]
    rows = 2 * FT
    count = len(own)
    pieces = [features[g] for g in groups]
    extras = [] if extra is None else [extra[g] for g in groups]
    all_rows = rows + SINK_ROWS * bool(extras)
    anywhere = pl.BlockSpec(memory_space=pl.ANY)
    whole = pl.BlockSpec(memory_space=pltpu.VMEM)

    def kernel(where_ref, *refs):
        piece_refs, refs = refs[: len(pieces)], refs[len(pieces) :]
        sides, refs = (refs[:count], refs[count : 2 * count]), refs[2 * count :]
        extra_refs, refs = refs[: len(extras)], refs[len(extras) :]
        out_refs, (feat, weights, sums, feat_sem, weight_sem) = refs[:-5], refs[-5:]
        x, core, z, y = where_ref[0], where_ref[1], where_ref[2], where_ref[3]

        copies = []
        for n, ref in enumerate(piece_refs):
            mine = [pltpu.make_async_copy(ref, feat.at[n, pl.ds(0, rows), :], feat_sem.at[n, 0])]
            if extras:
                mine.append(
                    pltpu.make_async_copy(
                        extra_refs[n], feat.at[n, pl.ds(rows, SINK_ROWS), :], feat_sem.at[n, 1]
                    )
                )
            for copy in mine:
                copy.start()
            copies.append(mine)
        for h in range(2):
            side = core if h == 0 else 1 - core
            for ref, row, bz, by in blocks_of(sides[h], z, y, side):
                ahead = lax.rem(bz - x + 4, 4)
                for n, g in enumerate(groups):

                    @pl.when(ahead == g)
                    def _():
                        pltpu.make_async_copy(
                            ref.at[pl.ds(row, 160), :],
                            weights.at[n, by, side],
                            weight_sem.at[n, by, side],
                        ).start()

        for n in range(len(groups)):
            for copy in copies[n]:
                copy.wait()
            for by in range(4):
                for side in range(2):
                    pltpu.make_async_copy(
                        sides[0][0].at[pl.ds(0, 160), :],
                        weights.at[n, by, side],
                        weight_sem.at[n, by, side],
                    ).wait()
            part = jnp.dot(
                feat[n], weights[n].reshape(FEAT, columns), preferred_element_type=jnp.float32
            )
            if n:
                part = part + sums[...]
            if n < len(groups) - 1:
                sums[...] = part
        out_refs[0][...] = part[:rows].astype(BF)
        if extras:
            out_refs[-1][...] = part[rows:].astype(BF)
        for ref, parts in zip(out_refs[1:], splits):
            at = 0
            for start, stop in parts:
                ref[:, at : at + stop - start] = out_refs[0][:, start:stop]
                at += stop - start

    shapes = [jax.ShapeDtypeStruct((rows, columns), BF)] + [
        jax.ShapeDtypeStruct((rows, sum(stop - start for start, stop in parts)), BF)
        for parts in splits
    ]
    if extras:
        shapes.append(jax.ShapeDtypeStruct((SINK_ROWS, columns), BF))
    return pl.pallas_call(
        kernel,
        out_shape=shapes,
        in_specs=[pl.BlockSpec(memory_space=pltpu.SMEM)]
        + [anywhere] * (len(pieces) + 2 * count + len(extras)),
        out_specs=[whole] * len(shapes),
        scratch_shapes=[
            pltpu.VMEM((len(groups), all_rows, FEAT), BF),
            pltpu.VMEM((len(groups), 4, 2, 160, columns), BF),
            pltpu.VMEM((all_rows, columns), jnp.float32),
            pltpu.SemaphoreType.DMA((len(pieces), 2)),
            pltpu.SemaphoreType.DMA((len(groups), 4, 2)),
        ],
        compiler_params=pltpu.CompilerParams(vmem_limit_bytes=VMEM_LIMIT),
        name="project",
    )(where, *pieces, *own, *other, *extras)


def attend_kernel(penalty_ref, query_ref, *refs):
    query = query_ref[...]
    lanes = HEAD_DIM
    keys, values = [], []
    for key_ref, value_ref in zip(refs[:4], refs[4:8]):
        for start in range(0, key_ref.shape[0], FT):
            keys.append((key_ref, start))
            values.append((value_ref, start))
    out_ref = refs[8]
    scores = []
    peak = None
    for f, (ref, start) in enumerate(keys):
        s = lax.dot_general(
            query,
            ref[start : start + FT, :],
            (((1,), (1,)), ((), ())),
            preferred_element_type=jnp.float32,
        )
        scores.append(s)
        top = jnp.maximum(
            jnp.maximum(s[:, :lanes], s[:, lanes : 2 * lanes]), s[:, 2 * lanes :]
        )
        if f >= 2:
            top = top - penalty_ref[f]
        peak = top if peak is None else jnp.maximum(peak, top)
    row_peak = jnp.max(peak, axis=1, keepdims=True) * EXP_SCALE
    totals = None
    blended = None
    for f, (ref, start) in enumerate(values):
        shift = row_peak if f < 2 else row_peak + penalty_ref[f]
        powers = jnp.exp2(scores[f] * EXP_SCALE - shift)
        part = powers[:, :lanes] + powers[:, lanes : 2 * lanes] + powers[:, 2 * lanes :]
        totals = part if totals is None else totals + part
        more = jnp.dot(
            powers.astype(BF), ref[start : start + FT, :], preferred_element_type=jnp.float32
        )
        blended = more if blended is None else blended + more
    total = jnp.sum(totals, axis=1, keepdims=True)
    out_ref[...] = (blended / total).astype(BF)


def attend(penalty, first, count, queries, key_value, sink, near, far):
    def columns(rows, begin):
        return pl.BlockSpec((rows, HEAD_DIM), lambda h: (0, begin + h))

    rows = 2 * FT
    return pl.pallas_call(
        attend_kernel,
        grid=(count,),
        out_shape=jax.ShapeDtypeStruct((rows, count * HEAD_DIM), BF),
        in_specs=[
            pl.BlockSpec(memory_space=pltpu.SMEM),
            columns(rows, first),
            columns(rows, first),
            columns(FT, first),
            columns(rows, 0),
            columns(rows, 0),
            columns(rows, 5 + first),
            columns(FT, 5 + first),
            columns(rows, count),
            columns(rows, count),
        ],
        out_specs=columns(rows, 0),
        compiler_params=pltpu.CompilerParams(vmem_limit_bytes=VMEM_LIMIT),
        name="attend",
    )(
        penalty,
        queries,
        key_value,
        sink,
        near,
        far,
        key_value,
        sink,
        near,
        far,
    )


def output(where, first, count, own, ring, weights, total, last):
    rows, width, step = 2 * FT, count * HEAD_DIM, 256
    totals = [] if total is None else [total]

    def kernel(where_ref, own_ref, left_ref, right_ref, far_ref, w_ref, *refs):
        total_refs, (out_ref, weight, sem) = refs[:-3], refs[-3:]
        x = where_ref[0]

        @pl.when(pl.program_id(0) == 0)
        def _():
            loads = []
            for g in range(4):
                begin = lax.rem(x + g, 4) * GROUP + first * HEAD_DIM
                loads.append(
                    pltpu.make_async_copy(
                        w_ref.at[:, pl.ds(pl.multiple_of(begin, HEAD_DIM), width)],
                        weight.at[g],
                        sem.at[g],
                    )
                )
            for load in loads:
                load.start()
            for load in loads:
                load.wait()

        result = None
        for g, ref in ((0, own_ref), (3, left_ref), (1, right_ref), (2, far_ref)):
            part = lax.dot_general(
                ref[...], weight[g], (((1,), (1,)), ((), ())), preferred_element_type=jnp.float32
            )
            result = part if result is None else result + part
        if totals:
            result = result + total_refs[0][...]
        out_ref[...] = result.astype(out_ref.dtype)

    block = pl.BlockSpec((step, FEAT), lambda i: (i, 0))
    piece = pl.BlockSpec((step, width), lambda i: (i, 0))
    return pl.pallas_call(
        kernel,
        grid=(rows // step,),
        out_shape=jax.ShapeDtypeStruct((rows, FEAT), BF if last else jnp.float32),
        in_specs=[pl.BlockSpec(memory_space=pltpu.SMEM)]
        + [piece] * 4
        + [pl.BlockSpec(memory_space=pl.ANY)]
        + [block] * len(totals),
        out_specs=block,
        scratch_shapes=[
            pltpu.VMEM((4, FEAT, width), BF),
            pltpu.SemaphoreType.DMA((4,)),
        ],
        compiler_params=pltpu.CompilerParams(vmem_limit_bytes=VMEM_LIMIT),
        name="output",
    )(where, own, *ring, weights, *totals)


def penalties(span, listed):
    ids = span * 2 + jnp.array([0, 1, 0, -2, -1, -4, -3], jnp.int32)
    ids = ids.at[2].set(0)
    found = jnp.any(ids[:, None] == listed[None, :], axis=1)
    slot = jnp.arange(7)
    allowed = (slot < 2) | (found & ((slot == 2) | (ids >= SINK)))
    return jnp.where(allowed, 0.0, ABSENT).astype(jnp.float32)


def local(tokens, w_query, w_key, w_value, w_out, frame_lists):
    span = lax.axis_index("seq")
    x = lax.axis_index("head")
    z, y, core = span // 8, span // 2 % 4, span % 2
    penalty = penalties(span, frame_lists[0])

    where = jnp.stack([x, core, z, y]).astype(jnp.int32)

    left, right, far = x_ring(tokens, core)
    sink_tokens = scatter_sink(tokens, span, far)
    features = {0: tokens, 1: right, 2: far, 3: left}
    kv_own = weight_ring(jnp.concatenate([w_key, w_value], axis=1))
    kv_other = [swap_cores(piece) for piece in kv_own]
    q_own, q_other = parity_gather(w_query)
    out_own, out_other = parity_gather(w_out.T)

    ends = [sum(SIZES[: n + 1]) for n in range(len(SIZES))]
    groups = [(end - size, size) for end, size in zip(ends, SIZES)]
    splits = [
        [
            (start * HEAD_DIM, (start + size) * HEAD_DIM),
            (GROUP + start * HEAD_DIM, GROUP + (start + size) * HEAD_DIM),
        ]
        for start, size in groups
    ]
    key_value, *sends, sink_part = project(
        where, features, sink_tokens, kv_own, kv_other, ring_blocks, (0, 1, 3, 2), splits
    )
    (queries,) = project(
        where, features, None, [q_own], [q_other], gather_blocks, (0, 1, 2, 3), ()
    )
    windows = []
    far = None
    for mine in sends:
        if far is not None:
            mine = after(mine, queries)
        far = spans_on(mine, 2)
        near = swap_cores(jnp.where(core == 0, mine, far))
        windows.append((near, far))
    sink = lax.all_gather(sink_part, "seq", axis=0, tiled=True)
    blocks = [out_own.reshape(16, 40, 2560), out_other.reshape(16, 40, 2560)]
    even = jnp.where(core == 0, blocks[0], blocks[1])
    odd = jnp.where(core == 0, blocks[1], blocks[0])
    out_weights = jnp.stack([even, odd], axis=1).reshape(FEAT, 2560)

    total = None
    ring = None
    for n, (start, size) in enumerate(groups):
        near, far = windows[n]
        attended = attend(
            penalty, start, size, queries, key_value, sink, near, far
        )
        if ring is not None:
            attended = after(attended, ring[0])
        ring = x_ring(attended, core)
        total = output(where, start, size, attended, ring, out_weights, total, n == len(groups) - 1)
    return total


def solution(mesh):
    placed = (
        P("seq", "head"),
        P("seq", "head"),
        P("seq", "head"),
        P("seq", "head"),
        P(None, ("head", "seq")),
        P("seq", None),
    )
    return jax.shard_map(
        local, mesh=mesh, in_specs=placed, out_specs=P("seq", "head"), check_vma=False
    )
```
